32 devices in a mesh: mol: 2 (over y), band: 8 (over z, x), grid: 2 (over core).
Axes of the slice: x: 2, y: 2, z: 4, core: 2. Of those that a mesh axis runs over, the one named last changes fastest.
Arguments:
- orbitals: bfloat16 [32, 373248], P(('mol', 'band'), 'grid'), parts along dimension 0, may hold values from -6 to 6
- group_order: int32 [32], P('mol'), parts along dimension 0, may hold values from 0 to 15, each once
- localizer: bfloat16 [2, 16, 16], P('mol'), parts along dimension 0, may hold values from -1.5 to 1.5
- bond_keep: int32 [32, 1], P('mol'), parts along dimension 0, may hold values 0 or 1
Outputs:
- localized: bfloat16 [32, 373248], P(('mol', 'band', 'grid')), parts along dimension 0
- exchange_term: bfloat16 [32, 373248], P(('mol', 'band', 'grid')), parts along dimension 0
The draws below stay inside these ranges and needn't reach their ends.
There are 2 independent parts, one for each index of `mol`. The reference program is written for one: setup_inputs(seed, part) draws one part's arguments, and reference() takes and returns one part's arrays. A program takes and returns all parts, laid end to end along the dimension named above; each array names one. Nothing has to cross between parts.
Inputs may be any that keep to these rules, and one draw needn't show every extreme that they name: A permutation; localization group g holds the orbitals group_order[g * 16 + a] for a below 16. `bond_keep`: 1 keeps a pair of orbitals, 0 screens it out.
All inputs are finite; a program needn't handle non-finite values.
Results may differ from the reference program's by a relative error of at most 0.0099.
Values may be sent and summed in bfloat16 or wider, within the bound.
A program may use at most 64 MiB of HBM per device.

```python
import math
import jax
import jax.numpy as jnp
from jax import lax

NG = 72
RADIUS = 1
ORBITALS = 16
GROUP = 16
NGROUPS = 1


def plant(drawn, key, low, largest):
    longest = drawn.shape.index(max(drawn.shape))
    spots = []
    for shift in (0, 1):
        where = [jax.random.randint(jax.random.fold_in(key, axis), (), 0, length) for axis, length in enumerate(drawn.shape)]
        where[longest] = (where[longest] + shift) % drawn.shape[longest]
        spots.append(tuple(where))
    return drawn.at[spots[0]].set(low).at[spots[1]].set(largest)


def steps_of(rng, dims, pieces, least, high):
    def one(position, parts):
        draws = jax.random.uniform(jax.random.fold_in(jax.random.fold_in(rng, 6), position), (parts,), jnp.float32, least / len(pieces), high / len(pieces))
        return jnp.repeat(jnp.exp(draws), dims[position] // parts).reshape((-1,) + (1,) * (len(dims) - position - 1))

    loudness = one(*pieces[0])
    for cut in pieces[1:]:
        loudness = loudness * one(*cut)
    return loudness


def normal_values(own_key, extent, spread, reach, shards=(), kind=jnp.bfloat16):
    values = jax.random.normal(own_key, extent, jnp.float32) * spread
    if len(shards) > 0:
        values = steps_of(own_key, extent, shards, -0.22, 0.18) * values
    return jnp.clip(values, min=-reach, max=reach).astype(kind)


def setup_inputs(seed: int = 0, part: int = 0) -> dict:
    key_list = jax.random.split(jax.random.key(seed), 5)
    part_splits = jax.random.split(jax.random.fold_in(key_list[4], part), 5)
    orbitals = normal_values(part_splits[0], (ORBITALS, NG * NG * NG), 1.0, 6.0, ((0, 8), (1, 2)))
    group_order = jax.random.permutation(part_splits[1], ORBITALS).astype(jnp.int32)
    localizer = normal_values(part_splits[2], (NGROUPS, GROUP, GROUP), GROUP ** -0.5, 1.5)
    bond_keep = plant((jax.random.randint(part_splits[3], (ORBITALS, RADIUS), 0, 4) < 3).astype(jnp.int32), jax.random.fold_in(part_splits[3], 1), 0, 1)
    return dict(orbitals=orbitals, group_order=group_order, localizer=localizer, bond_keep=bond_keep)


screening = 0.0625


def round_half(values):
    return lax.optimization_barrier(values.astype(jnp.bfloat16)).astype(jnp.float32)


def phase_angles(row_count, column_total):
    first_index = jnp.arange(row_count, dtype=jnp.int32)[:, None]
    second_index = jnp.arange(column_total, dtype=jnp.int32)[None, :]
    return (2.0 * math.pi / NG) * ((first_index * second_index) % NG).astype(jnp.float32)


def build_tables():
    half_count = NG // 2 + 1
    along_x = phase_angles(half_count, NG)
    x_table = jnp.stack([jnp.cos(along_x), -jnp.sin(along_x)])
    square = phase_angles(NG, NG)
    cosine_table = jnp.cos(square)
    sine_table = jnp.sin(square)
    forward_depth_axis = jnp.concatenate([jnp.concatenate([cosine_table, -sine_table], axis=1), jnp.concatenate([sine_table, cosine_table], axis=1)], axis=0)
    inverse_z = jnp.concatenate([jnp.concatenate([cosine_table, sine_table], axis=1), jnp.concatenate([-sine_table, cosine_table], axis=1)], axis=0)
    y_table = jnp.concatenate([cosine_table, sine_table], axis=0)
    half_angle = (math.pi / NG) * jnp.arange(NG, dtype=jnp.int32).astype(jnp.float32)
    symbol = 4.0 * jnp.sin(half_angle) ** 2
    denominator = screening + symbol[:half_count, None, None] + symbol[None, :, None] + symbol[None, None, :]
    x_index = jnp.arange(half_count, dtype=jnp.int32)
    weight = jnp.where((x_index == 0) | (x_index == NG // 2), 1.0, 2.0).astype(jnp.float32) / float(NG * NG * NG)
    kernel = weight[:, None, None] / denominator
    anchor = jnp.zeros((half_count, NG, NG), jnp.float32).at[0, 0, 0].set(1.0)
    kernel = kernel * (1.0 - anchor)
    kernel = jnp.concatenate([kernel, kernel], axis=2)
    return (round_half(x_table), round_half(forward_depth_axis), round_half(inverse_z), round_half(y_table), kernel)


def mix_along_y(spectrum, y_table, phase_sign):
    products = jnp.einsum("jy,kyc->kjc", y_table, spectrum, precision=lax.Precision.HIGHEST)
    cos_part = products[:, :NG]
    sin_part = products[:, NG:]
    real_part = cos_part[:, :, :NG] - phase_sign * sin_part[:, :, NG:]
    imag_part = cos_part[:, :, NG:] + phase_sign * sin_part[:, :, :NG]
    return jnp.concatenate([real_part, imag_part], axis=2)


def potential(left_field, right_field, tables):
    x_table, forward_depth_axis, inverse_z, y_table, kernel = tables
    half_count = x_table.shape[1]
    density = round_half(left_field * right_field)
    section_field = jnp.einsum("pkx,xyz->kypz", x_table, density, precision=lax.Precision.HIGHEST)
    section_field = round_half(section_field.reshape(half_count, NG, 2 * NG))
    section_field = jnp.dot(section_field.reshape(half_count * NG, 2 * NG), forward_depth_axis, precision=lax.Precision.HIGHEST, preferred_element_type=jnp.float32)
    section_field = round_half(section_field.reshape(half_count, NG, 2 * NG))
    section_field = round_half(mix_along_y(section_field, y_table, -1.0) * kernel)
    section_field = round_half(mix_along_y(section_field, y_table, 1.0))
    section_field = jnp.dot(section_field.reshape(half_count * NG, 2 * NG), inverse_z, precision=lax.Precision.HIGHEST, preferred_element_type=jnp.float32)
    section_field = round_half(section_field.reshape(half_count, NG, 2, NG))
    return jnp.einsum("pkx,kypz->xyz", x_table, section_field, precision=lax.Precision.HIGHEST)


def reference(orbitals, group_order, localizer, bond_keep):
    orbit_count = orbitals.shape[0]
    group_count = localizer.shape[0]
    group_width = localizer.shape[1]
    grouped_orbitals = orbitals[group_order].astype(jnp.float32).reshape(group_count, group_width, -1)
    rotated_field = jnp.einsum("iek,ikv->iev", localizer.astype(jnp.float32), grouped_orbitals, precision=lax.Precision.HIGHEST)
    rotated_field = rotated_field.reshape(orbit_count, -1).astype(jnp.bfloat16)
    localized = jnp.zeros_like(rotated_field).at[group_order].set(rotated_field)
    tables = build_tables()
    orbit_floats = localized.astype(jnp.float32)

    def exchange_row(orbital_index):
        own_float = orbit_floats[orbital_index].reshape(NG, NG, NG)
        exchange_sum = potential(own_float, own_float, tables) * own_float
        for offset in range(1, RADIUS + 1):
            lower_index = (orbital_index - offset) % orbit_count
            upper_partner_index = (orbital_index + offset) % orbit_count
            lower_float = orbit_floats[lower_index].reshape(NG, NG, NG)
            upper_partner_float = orbit_floats[upper_partner_index].reshape(NG, NG, NG)
            lower_flag = bond_keep[orbital_index, offset - 1].astype(jnp.float32)
            upper_flag = bond_keep[upper_partner_index, offset - 1].astype(jnp.float32)
            exchange_sum = exchange_sum + lower_flag * potential(own_float, lower_float, tables) * lower_float
            exchange_sum = exchange_sum + upper_flag * potential(own_float, upper_partner_float, tables) * upper_partner_float
        return exchange_sum.reshape(-1).astype(jnp.bfloat16)

    exchange_term = lax.map(exchange_row, jnp.arange(orbit_count, dtype=jnp.int32))
    return (localized, exchange_term)
```

```python
import math

import jax
import jax.numpy as jnp
import numpy as np
from jax import lax
from jax.experimental import pallas as pl
from jax.experimental.pallas import tpu as pltpu
from jax.sharding import PartitionSpec as P

NG = 72
LANES = 128
HALF = NG // 2 + 1
KPAD = 40
PAIRS = KPAD // 2
GROUP_K = 4
GROUP_Y = 4

screening = 0.0625


def from_behind(shard, axis, by):
    peers = lax.axis_size(axis)
    return lax.ppermute(shard, axis, [(i, (i + by) % peers) for i in range(peers)])


def build_tables():
    a = np.arange(NG)
    angle = 2.0 * math.pi / NG * ((a[:, None] * a[None, :]) % NG)
    cos = np.cos(angle)
    sin = np.sin(angle)
    x_forward = np.zeros((2 * KPAD, NG))
    x_forward[:HALF] = cos[:HALF]
    x_forward[KPAD : KPAD + HALF] = -sin[:HALF]
    x_inverse = x_forward.T
    z_forward = np.zeros((2 * LANES, 2 * LANES))
    z_inverse = np.zeros((2 * LANES, 2 * LANES))
    for table, sign in ((z_forward, 1.0), (z_inverse, -1.0)):
        table[:NG, :NG] = cos
        table[:NG, LANES : LANES + NG] = -sign * sin
        table[LANES : LANES + NG, :NG] = sign * sin
        table[LANES : LANES + NG, LANES : LANES + NG] = cos
    y_forward = np.block([[cos, sin], [-sin, cos]])
    y_inverse = np.block([[cos, -sin], [sin, cos]])
    symbol = 4.0 * np.sin(math.pi / NG * a) ** 2
    denominator = (
        screening + symbol[:HALF, None, None] + symbol[None, :, None] + symbol[None, None, :]
    )
    weight = np.where((a[:HALF] == 0) | (a[:HALF] == NG // 2), 1.0, 2.0) / float(NG**3)
    kernel = weight[:, None, None] / denominator
    kernel[0, 0, 0] = 0.0
    padded = np.zeros((KPAD, NG, LANES))
    padded[:HALF, :, :NG] = kernel
    padded = padded.reshape(PAIRS, 2, NG, LANES).transpose(0, 2, 1, 3)
    padded = padded.reshape(PAIRS, NG, 2 * LANES)
    narrow = [
        jnp.asarray(t.astype(np.float32)).astype(jnp.bfloat16)
        for t in (x_forward, x_inverse, z_forward, z_inverse, y_forward, y_inverse)
    ]
    return (*narrow, jnp.asarray(padded.astype(np.float32)))


def dot(a, b):
    return jnp.dot(a, b, preferred_element_type=jnp.float32)


def forward_x(grid, part_re, part_im, xf):
    table = xf[...]

    @pl.loop(0, NG // (2 * GROUP_Y))
    def _(step):
        for inner in range(GROUP_Y):
            y = (step * GROUP_Y + inner) * 2
            plane = jnp.concatenate(
                [grid[pl.ds(y + i, NG, stride=NG), :] for i in range(2)], axis=1
            ).astype(jnp.bfloat16)
            out = dot(table, plane)
            for i in range(2):
                lanes = slice(i * LANES, (i + 1) * LANES)
                part_re[pl.ds(y + i, KPAD, stride=NG), :] = out[:KPAD, lanes]
                part_im[pl.ds(y + i, KPAD, stride=NG), :] = out[KPAD:, lanes]


def restack(block):
    top, low = block[:NG], block[NG:]
    return jnp.concatenate(
        [
            jnp.concatenate([top[:, :LANES], low[:, :LANES]], axis=1),
            jnp.concatenate([top[:, LANES:], low[:, LANES:]], axis=1),
        ],
        axis=0,
    ).astype(jnp.bfloat16)


def middle(part_re, part_im, zf, zi, yf, yi, kern):
    @pl.loop(0, PAIRS // GROUP_K)
    def _(step):
        pairs = [step * GROUP_K + inner for inner in range(GROUP_K)]
        rows = [pl.ds(pl.multiple_of(p * 2 * NG, 8), 2 * NG) for p in pairs]
        work = [
            jnp.concatenate([part_re[r, :], part_im[r, :]], axis=1).astype(jnp.bfloat16)
            for r in rows
        ]
        work = [restack(dot(w, zf[...])) for w in work]
        third = []
        for w, p in zip(work, pairs):
            t = dot(yf[...], w)
            scale = kern[p]
            third.append(
                jnp.concatenate([t[:NG] * scale, t[NG:] * scale], axis=0).astype(jnp.bfloat16)
            )
        work = [restack(dot(yi[...], t)) for t in third]
        for w, r in zip(work, rows):
            out = dot(w, zi[...])
            part_re[r, :] = out[:, :LANES]
            part_im[r, :] = out[:, LANES:]


def inverse_x(grid, part_re, part_im, xi):
    table = xi[...]

    @pl.loop(0, NG // (2 * GROUP_Y))
    def _(step):
        for inner in range(GROUP_Y):
            y = (step * GROUP_Y + inner) * 2
            plane = jnp.concatenate(
                [
                    jnp.concatenate(
                        [
                            part_re[pl.ds(y + i, KPAD, stride=NG), :],
                            part_im[pl.ds(y + i, KPAD, stride=NG), :],
                        ],
                        axis=0,
                    )
                    for i in range(2)
                ],
                axis=1,
            ).astype(jnp.bfloat16)
            out = dot(table, plane)
            for i in range(2):
                grid[pl.ds(y + i, NG, stride=NG), :] = out[:, i * LANES : (i + 1) * LANES]


def self_kernel(own, xf, xi, zf, zi, yf, yi, kern, term, grid, part_re, part_im):
    @pl.loop(0, NG)
    def _(x):
        rows = pl.ds(pl.multiple_of(x * NG, 8), NG)
        value = own[rows, :].astype(jnp.float32)
        grid[rows, :] = jnp.zeros((NG, LANES), jnp.float32)
        grid[rows, :NG] = value * value

    forward_x(grid, part_re, part_im, xf)
    middle(part_re, part_im, zf, zi, yf, yi, kern)
    inverse_x(grid, part_re, part_im, xi)

    @pl.loop(0, NG)
    def _(x):
        rows = pl.ds(pl.multiple_of(x * NG, 8), NG)
        term[rows, :] = grid[rows, :NG] * own[rows, :].astype(jnp.float32)


def pair_kernel(
    flag, own, lower, so_far, xf, xi, zf, zi, yf, yi, kern, term, sent, grid, part_re, part_im
):
    @pl.loop(0, NG)
    def _(x):
        rows = pl.ds(pl.multiple_of(x * NG, 8), NG)
        value = own[rows, :].astype(jnp.float32) * lower[rows, :].astype(jnp.float32)
        grid[rows, :] = jnp.zeros((NG, LANES), jnp.float32)
        grid[rows, :NG] = value

    forward_x(grid, part_re, part_im, xf)
    middle(part_re, part_im, zf, zi, yf, yi, kern)
    inverse_x(grid, part_re, part_im, xi)
    keep = flag[0]

    @pl.loop(0, NG)
    def _(x):
        rows = pl.ds(pl.multiple_of(x * NG, 8), NG)
        field = grid[rows, :NG] * keep
        term[rows, :] = so_far[rows, :] + field * lower[rows, :].astype(jnp.float32)
        sent[rows, :] = (field * own[rows, :].astype(jnp.float32)).astype(jnp.bfloat16)


SCRATCH = [
    pltpu.VMEM((NG * NG, LANES), jnp.float32),
    pltpu.VMEM((KPAD * NG, LANES), jnp.float32),
    pltpu.VMEM((KPAD * NG, LANES), jnp.float32),
]
COST = pl.CostEstimate(flops=2 * 300_000_000, bytes_accessed=6_000_000, transcendentals=0)
PARAMS = pltpu.CompilerParams(vmem_limit_bytes=40 * 2**20)


def in_vmem(count):
    return [pl.BlockSpec(memory_space=pltpu.VMEM)] * count


def self_term(own, tables):
    return pl.pallas_call(
        self_kernel,
        out_shape=jax.ShapeDtypeStruct(own.shape, jnp.float32),
        in_specs=in_vmem(1 + len(tables)),
        out_specs=pl.BlockSpec(memory_space=pltpu.VMEM),
        scratch_shapes=SCRATCH,
        compiler_params=PARAMS,
        cost_estimate=COST,
        name="self_term",
    )(own, *tables)


def pair_term(flag, own, lower, so_far, tables):
    return pl.pallas_call(
        pair_kernel,
        out_shape=(
            jax.ShapeDtypeStruct(own.shape, jnp.float32),
            jax.ShapeDtypeStruct(own.shape, jnp.bfloat16),
        ),
        in_specs=[pl.BlockSpec(memory_space=pltpu.SMEM)] + in_vmem(3 + len(tables)),
        out_specs=tuple(in_vmem(2)),
        scratch_shapes=SCRATCH,
        compiler_params=PARAMS,
        cost_estimate=COST,
        name="pair_term",
    )(flag, own, lower, so_far, *tables)


def body(orbitals, group_order, localizer, bond_keep):
    pieces = lax.all_to_all(orbitals, "band", split_axis=1, concat_axis=0, tiled=True)
    orbit_count = pieces.shape[0]
    group_count = localizer.shape[0]
    group_width = localizer.shape[1]
    grouped_orbitals = pieces[group_order].reshape(group_count, group_width, pieces.shape[1])
    rotated_field = jnp.einsum(
        "iek,ikv->iev", localizer, grouped_orbitals, preferred_element_type=jnp.float32
    )
    rotated_field = rotated_field.reshape(orbit_count, pieces.shape[1]).astype(jnp.bfloat16)
    ordered = jnp.zeros_like(rotated_field).at[group_order].set(rotated_field)
    localized = lax.all_to_all(
        lax.all_to_all(ordered, "band", split_axis=0, concat_axis=1, tiled=True),
        "grid",
        split_axis=0,
        concat_axis=1,
        tiled=True,
    )
    position = lax.axis_index("band") * lax.axis_size("grid") + lax.axis_index("grid")
    tables = build_tables()
    flag = bond_keep[position].astype(jnp.float32)[:1]
    own = localized[0].reshape(NG * NG, NG)
    lower = from_behind(own, ("band", "grid"), 1)
    so_far = self_term(own, tables)
    so_far, sent = pair_term(flag, own, lower, so_far, tables)
    returned = from_behind(sent, ("band", "grid"), -1)
    total = (so_far + returned.astype(jnp.float32)).astype(jnp.bfloat16)
    return (localized, total.reshape(1, -1))


def solution(mesh):
    in_specs = (P(("mol", "band"), "grid"), P("mol"), P("mol", None, None), P("mol", None))
    out_specs = (P(("mol", "band", "grid"), None), P(("mol", "band", "grid"), None))
    return jax.shard_map(body, mesh=mesh, in_specs=in_specs, out_specs=out_specs, check_vma=False)
```

```python
import functools
import math

import jax
import jax.numpy as jnp
import numpy as np
from jax import lax
from jax.experimental import pallas as pl
from jax.experimental.pallas import tpu as pltpu
from jax.sharding import PartitionSpec as P

NG = 72
LANES = 128
HALF = NG // 2 + 1
KPAD = 40
PAIRS = KPAD // 2
GROUP_K = 4
GROUP_Y = 4
PER_FLAT = 9
PER_ROWS = 16
GROUPS = NG**3 // (2 * PER_FLAT * LANES)

screening = 0.0625


def from_behind(shard, axis, by):
    peers = lax.axis_size(axis)
    return lax.ppermute(shard, axis, [(i, (i + by) % peers) for i in range(peers)])


def build_tables():
    a = np.arange(NG)
    angle = 2.0 * math.pi / NG * ((a[:, None] * a[None, :]) % NG)
    cos = np.cos(angle)
    sin = np.sin(angle)
    x_forward = np.zeros((2 * KPAD, NG))
    x_forward[:HALF] = cos[:HALF]
    x_forward[KPAD : KPAD + HALF] = -sin[:HALF]
    x_inverse = x_forward.T
    z_forward = np.zeros((2 * LANES, 2 * LANES))
    z_inverse = np.zeros((2 * LANES, 2 * LANES))
    for table, sign in ((z_forward, 1.0), (z_inverse, -1.0)):
        table[:NG, :NG] = cos
        table[:NG, LANES : LANES + NG] = -sign * sin
        table[LANES : LANES + NG, :NG] = sign * sin
        table[LANES : LANES + NG, LANES : LANES + NG] = cos
    y_forward = np.block([[cos, sin], [-sin, cos]])
    y_inverse = np.block([[cos, -sin], [sin, cos]])
    symbol = 4.0 * np.sin(math.pi / NG * a) ** 2
    denominator = (
        screening + symbol[:HALF, None, None] + symbol[None, :, None] + symbol[None, None, :]
    )
    weight = np.where((a[:HALF] == 0) | (a[:HALF] == NG // 2), 1.0, 2.0) / float(NG**3)
    kernel = weight[:, None, None] / denominator
    kernel[0, 0, 0] = 0.0
    padded = np.zeros((KPAD, NG, LANES))
    padded[:HALF, :, :NG] = kernel
    padded = padded.reshape(PAIRS, 2, NG, LANES).transpose(0, 2, 1, 3)
    padded = padded.reshape(PAIRS, NG, 2 * LANES)
    narrow = [
        jnp.asarray(t.astype(np.float32)).astype(jnp.bfloat16)
        for t in (x_forward, x_inverse, z_forward, z_inverse, y_forward, y_inverse)
    ]
    return (*narrow, jnp.asarray(padded.astype(np.float32)))


def dot(a, b):
    return jnp.dot(a, b, preferred_element_type=jnp.float32)


def forward_x(grid, part_re, part_im, xf):
    table = xf[...]

    @pl.loop(0, NG // (2 * GROUP_Y))
    def _(step):
        for inner in range(GROUP_Y):
            y = (step * GROUP_Y + inner) * 2
            plane = jnp.concatenate(
                [grid[pl.ds(y + i, NG, stride=NG), :] for i in range(2)], axis=1
            ).astype(jnp.bfloat16)
            out = dot(table, plane)
            for i in range(2):
                lanes = slice(i * LANES, (i + 1) * LANES)
                part_re[pl.ds(y + i, KPAD, stride=NG), :] = out[:KPAD, lanes]
                part_im[pl.ds(y + i, KPAD, stride=NG), :] = out[KPAD:, lanes]


def restack(block):
    top, low = block[:NG], block[NG:]
    return jnp.concatenate(
        [
            jnp.concatenate([top[:, :LANES], low[:, :LANES]], axis=1),
            jnp.concatenate([top[:, LANES:], low[:, LANES:]], axis=1),
        ],
        axis=0,
    ).astype(jnp.bfloat16)


def middle(part_re, part_im, zf, zi, yf, yi, kern):
    @pl.loop(0, PAIRS // GROUP_K)
    def _(step):
        pairs = [step * GROUP_K + inner for inner in range(GROUP_K)]
        rows = [pl.ds(pl.multiple_of(p * 2 * NG, 8), 2 * NG) for p in pairs]
        work = [
            jnp.concatenate([part_re[r, :], part_im[r, :]], axis=1).astype(jnp.bfloat16)
            for r in rows
        ]
        work = [restack(dot(w, zf[...])) for w in work]
        third = []
        for w, p in zip(work, pairs):
            t = dot(yf[...], w)
            scale = kern[p]
            third.append(
                jnp.concatenate([t[:NG] * scale, t[NG:] * scale], axis=0).astype(jnp.bfloat16)
            )
        work = [restack(dot(yi[...], t)) for t in third]
        for w, r in zip(work, rows):
            out = dot(w, zi[...])
            part_re[r, :] = out[:, :LANES]
            part_im[r, :] = out[:, LANES:]


def inverse_x(grid, part_re, part_im, xi):
    table = xi[...]

    @pl.loop(0, NG // (2 * GROUP_Y))
    def _(step):
        for inner in range(GROUP_Y):
            y = (step * GROUP_Y + inner) * 2
            plane = jnp.concatenate(
                [
                    jnp.concatenate(
                        [
                            part_re[pl.ds(y + i, KPAD, stride=NG), :],
                            part_im[pl.ds(y + i, KPAD, stride=NG), :],
                        ],
                        axis=0,
                    )
                    for i in range(2)
                ],
                axis=1,
            ).astype(jnp.bfloat16)
            out = dot(table, plane)
            for i in range(2):
                grid[pl.ds(y + i, NG, stride=NG), :] = out[:, i * LANES : (i + 1) * LANES]


def widen(flat, wide, rows_per_half):
    lane = lax.broadcasted_iota(jnp.int32, (GROUPS, LANES), 1)

    @pl.loop(0, 2)
    def _(half):
        source = half * rows_per_half
        target = half * (NG * NG // 2)
        for r in range(PER_ROWS):
            first, offset = divmod(r * NG, LANES)
            value = flat[pl.ds(source + first, GROUPS, stride=PER_FLAT), :]
            if offset + NG > LANES:
                after = flat[pl.ds(source + first + 1, GROUPS, stride=PER_FLAT), :]
                value = jnp.where(lane >= offset, value, after)
            if offset:
                value = pltpu.roll(value, LANES - offset, 1)
            wide[pl.ds(target + r, GROUPS, stride=PER_ROWS), :] = value


def narrow(wide, flat):
    lane = lax.broadcasted_iota(jnp.int32, (GROUPS, LANES), 1)

    @pl.loop(0, 2)
    def _(half):
        source = half * (NG * NG // 2)
        target = half * (GROUPS * PER_FLAT)
        for s in range(PER_FLAT):
            first, offset = divmod(s * LANES, NG)
            value = None
            start = -offset
            row = first
            while start < LANES:
                piece = wide[pl.ds(source + row, GROUPS, stride=PER_ROWS), :]
                if start % LANES:
                    piece = pltpu.roll(piece, start % LANES, 1)
                value = piece if value is None else jnp.where(lane >= start, piece, value)
                start += NG
                row += 1
            flat[pl.ds(target + s, GROUPS, stride=PER_FLAT), :] = value


def unpack(packed, flat):
    halves, pieces, rows, _ = packed.shape

    @pl.loop(0, halves)
    def _(half):
        @pl.loop(0, pieces)
        def _(piece):
            start = pl.multiple_of((half * pieces + piece) * rows, 16)
            flat[pl.ds(start, rows), :] = packed[half, piece].astype(jnp.float32)


def planes(work):
    @pl.loop(0, NG)
    def _(x):
        work(pl.ds(pl.multiple_of(x * NG, 8), NG))


def transform(grid, part_re, part_im, tables):
    xf, xi, zf, zi, yf, yi, kern = tables
    forward_x(grid, part_re, part_im, xf)
    middle(part_re, part_im, zf, zi, yf, yi, kern)
    inverse_x(grid, part_re, part_im, xi)


def self_kernel(packed, *refs):
    tables, (term, own, flat, value, grid, part_re, part_im) = refs[:7], refs[7:]
    unpack(packed, flat)
    widen(flat, value, packed.shape[1] * packed.shape[2])

    @planes
    def _(rows):
        u = value[rows, :]
        own[rows, :] = u.astype(jnp.bfloat16)
        grid[rows, :] = u * u

    transform(grid, part_re, part_im, tables)

    @planes
    def _(rows):
        term[rows, :] = grid[rows, :] * value[rows, :]


def pair_kernel(flags, own, so_far, lower, upper, *refs):
    tables, (out, flat, value, grid, part_re, part_im, total) = refs[:7], refs[7:]
    for which, packed in enumerate((lower, upper)):
        unpack(packed, flat)
        widen(flat, value, packed.shape[1] * packed.shape[2])

        @planes
        def _(rows):
            grid[rows, :] = own[rows, :].astype(jnp.float32) * value[rows, :]

        transform(grid, part_re, part_im, tables)
        keep = flags[which]
        before = so_far if which == 0 else total

        @planes
        def _(rows):
            total[rows, :] = before[rows, :] + grid[rows, :] * keep * value[rows, :]

    narrow(total, flat)
    out[...] = flat[: out.shape[0], :].astype(jnp.bfloat16)


def exchange_scratch(flat_rows):
    return [
        pltpu.VMEM((flat_rows, LANES), jnp.float32),
        pltpu.VMEM((NG * NG, LANES), jnp.float32),
        pltpu.VMEM((NG * NG, LANES), jnp.float32),
        pltpu.VMEM((KPAD * NG, LANES), jnp.float32),
        pltpu.VMEM((KPAD * NG, LANES), jnp.float32),
    ]


def in_vmem(count):
    return [pl.BlockSpec(memory_space=pltpu.VMEM)] * count


def cost(count):
    return pl.CostEstimate(
        flops=count * 2_000_000_000, bytes_accessed=8_000_000, transcendentals=0
    )


PARAMS = pltpu.CompilerParams(vmem_limit_bytes=48 * 2**20)


def self_term(packed, tables):
    flat_rows = packed.size // LANES
    return pl.pallas_call(
        self_kernel,
        out_shape=(
            jax.ShapeDtypeStruct((NG * NG, LANES), jnp.float32),
            jax.ShapeDtypeStruct((NG * NG, LANES), jnp.bfloat16),
        ),
        in_specs=in_vmem(1 + len(tables)),
        out_specs=tuple(in_vmem(2)),
        scratch_shapes=exchange_scratch(flat_rows),
        compiler_params=PARAMS,
        cost_estimate=cost(1),
        name="self_term",
    )(packed, *tables)


def pair_terms(flags, own, so_far, lower, upper, tables):
    flat_rows = lower.size // LANES
    return pl.pallas_call(
        pair_kernel,
        out_shape=jax.ShapeDtypeStruct((NG**3 // LANES, LANES), jnp.bfloat16),
        in_specs=[pl.BlockSpec(memory_space=pltpu.SMEM)] + in_vmem(4 + len(tables)),
        out_specs=pl.BlockSpec(memory_space=pltpu.VMEM),
        scratch_shapes=exchange_scratch(flat_rows)
        + [pltpu.VMEM((NG * NG, LANES), jnp.float32)],
        compiler_params=PARAMS,
        cost_estimate=cost(2),
        name="pair_terms",
    )(flags, own, so_far, lower, upper, *tables)


def localize_kernel(
    bands, cores, chunks, orb, mix, loc, recv, mixed, landed, whole, blended, sems, out_sems
):
    mol = lax.axis_index("mol")
    band = lax.axis_index("band")
    core = lax.axis_index("grid")
    me = band * cores + core
    devices = bands * cores
    held = orb.shape[0]
    orbits = held * bands
    rows = orb.shape[2] // chunks
    mesh_id = pl.DeviceIdType.MESH

    barrier = pltpu.get_barrier_semaphore()

    @pl.loop(1, devices)
    def _(k):
        peer = lax.rem(me + k, devices)
        pl.semaphore_signal(
            barrier,
            inc=1,
            device_id=(mol, peer // cores, lax.rem(peer, cores)),
            device_id_type=mesh_id,
        )

    pl.semaphore_wait(barrier, devices - 1)

    def first(q, k, sender):
        span = pl.ds(q * rows, rows)
        peer = lax.rem(band + k, bands)
        return pltpu.make_async_remote_copy(
            src_ref=orb.at[:, peer, span],
            dst_ref=recv.at[q, sender],
            send_sem=sems.at[0, q, peer],
            recv_sem=sems.at[1, q, sender],
            device_id=(mol, peer, core),
            device_id_type=mesh_id,
        )

    def second(q, k, sender):
        peer = lax.rem(me + k, devices)
        sender_band, sender_core = sender // cores, lax.rem(sender, cores)
        return pltpu.make_async_remote_copy(
            src_ref=mixed.at[q, peer],
            dst_ref=landed.at[sender_core, sender_band, pl.ds(q * rows, rows)],
            send_sem=out_sems.at[0, q, peer],
            recv_sem=out_sems.at[1, q, sender],
            device_id=(mol, peer // cores, lax.rem(peer, cores)),
            device_id_type=mesh_id,
        )

    for q in range(chunks):

        @pl.loop(1, bands)
        def _(k):
            first(q, k, band).start()

    for q in range(chunks):
        for h in range(held):
            start = pl.multiple_of((band * held + h) * rows, 16)
            whole[pl.ds(start, rows), :] = orb[h, band, pl.ds(q * rows, rows), :].astype(
                jnp.float32
            )

        @pl.loop(1, bands)
        def _(k):
            sender = lax.rem(band + k, bands)
            first(q, k, sender).wait_recv()
            for h in range(held):
                start = pl.multiple_of((sender * held + h) * rows, 16)
                whole[pl.ds(start, rows), :] = recv[q, sender, h].astype(jnp.float32)

        table = mix[...]

        @pl.loop(0, rows // 8)
        def _(step):
            for inner in range(4):
                r = step * 8 + inner * 2
                block = jnp.concatenate(
                    [whole[pl.ds(r + i, orbits, stride=rows), :] for i in range(2)], axis=1
                ).astype(jnp.bfloat16)
                out = dot(table, block)
                for i in range(2):
                    blended[pl.ds(r + i, orbits, stride=rows), :] = out[
                        :, i * LANES : (i + 1) * LANES
                    ]

        @pl.loop(0, orbits)
        def _(i):
            start = pl.multiple_of(i * rows, 16)
            mixed[q, i] = blended[pl.ds(start, rows), :].astype(jnp.bfloat16)

        @pl.loop(1, devices)
        def _(k):
            second(q, k, me).start()

        landed[core, band, pl.ds(q * rows, rows)] = mixed[q, me]

    for q in range(chunks):

        @pl.loop(1, devices)
        def _(k):
            second(q, k, lax.rem(me + k, devices)).wait_recv()

    loc[...] = landed[...]
    for q in range(chunks):

        @pl.loop(1, bands)
        def _(k):
            first(q, k, band).wait_send()

        @pl.loop(1, devices)
        def _(k):
            second(q, k, me).wait_send()


def localize(orb, mix, cores):
    held, bands, rows, _ = orb.shape
    orbits = held * bands
    chunks = 3 if rows % 48 == 0 else 1
    part = rows // chunks
    return pl.pallas_call(
        functools.partial(localize_kernel, bands, cores, chunks),
        out_shape=jax.ShapeDtypeStruct((cores, bands, rows, LANES), jnp.bfloat16),
        in_specs=in_vmem(2),
        out_specs=pl.BlockSpec(memory_space=pltpu.VMEM),
        scratch_shapes=[
            pltpu.VMEM((chunks, bands, held, part, LANES), jnp.bfloat16),
            pltpu.VMEM((chunks, orbits, part, LANES), jnp.bfloat16),
            pltpu.VMEM((cores, bands, rows, LANES), jnp.bfloat16),
            pltpu.VMEM((orbits * part, LANES), jnp.float32),
            pltpu.VMEM((orbits * part, LANES), jnp.float32),
            pltpu.SemaphoreType.DMA((2, chunks, bands)),
            pltpu.SemaphoreType.DMA((2, chunks, bands * cores)),
        ],
        compiler_params=pltpu.CompilerParams(
            collective_id=0, has_side_effects=True, vmem_limit_bytes=32 * 2**20
        ),
        name="localize",
    )(orb, mix)


def mixing_matrix(group_order, localizer):
    groups, width, _ = localizer.shape
    orbits = group_order.shape[0]
    pick = (group_order[:, None] == jnp.arange(orbits, dtype=jnp.int32)[None, :]).astype(
        jnp.bfloat16
    )
    pick = pick.reshape(groups, width, orbits)
    half = jnp.einsum("gab,gbj->gaj", localizer, pick, preferred_element_type=jnp.float32)
    return jnp.einsum(
        "gai,gaj->ij", pick, half.astype(jnp.bfloat16), preferred_element_type=jnp.float32
    ).astype(jnp.bfloat16)


def body(orbitals, group_order, localizer, bond_keep):
    bands = lax.axis_size("band")
    cores = lax.axis_size("grid")
    devices = bands * cores
    held, span = orbitals.shape
    flat_rows = span // LANES
    rows = -(-flat_rows // (bands * 16)) * 16
    orb = orbitals.reshape(held, flat_rows, LANES)
    orb = jnp.pad(orb, ((0, 0), (0, rows * bands - flat_rows), (0, 0)))
    orb = orb.reshape(held, bands, rows, LANES)
    packed = localize(orb, mixing_matrix(group_order, localizer), cores)
    position = lax.axis_index("band") * cores + lax.axis_index("grid")
    tables = build_tables()
    flags = jnp.stack(
        [bond_keep[position, 0], bond_keep[lax.rem(position + 1, devices), 0]]
    ).astype(jnp.float32)
    lower = from_behind(packed, ("band", "grid"), 1)
    upper = from_behind(packed, ("band", "grid"), -1)
    so_far, own = self_term(packed, tables)
    localized = packed.reshape(cores, bands * rows, LANES)[:, :flat_rows].reshape(1, -1)
    total = pair_terms(flags, own, so_far, lower, upper, tables)
    return (localized, total.reshape(1, -1))


def solution(mesh):
    in_specs = (P(("mol", "band"), "grid"), P("mol"), P("mol", None, None), P("mol", None))
    out_specs = (P(("mol", "band", "grid"), None), P(("mol", "band", "grid"), None))
    return jax.shard_map(body, mesh=mesh, in_specs=in_specs, out_specs=out_specs, check_vma=False)
```

```python
import functools
import math

import jax
import jax.numpy as jnp
import numpy as np
from jax import lax
from jax.experimental import pallas as pl
from jax.experimental.pallas import tpu as pltpu
from jax.sharding import PartitionSpec as P

NG = 72
LANES = 128
HALF = NG // 2 + 1
KPAD = 40
PAIRS = KPAD // 2
GROUP_K = 5
GROUP_Y = 6
PER_FLAT = 9
PER_ROWS = 16
GROUPS = NG**3 // (2 * PER_FLAT * LANES)

screening = 0.0625


def from_behind(shard, axis, by):
    peers = lax.axis_size(axis)
    return lax.ppermute(shard, axis, [(i, (i + by) % peers) for i in range(peers)])


def build_tables():
    a = np.arange(NG)
    angle = 2.0 * math.pi / NG * ((a[:, None] * a[None, :]) % NG)
    cos = np.cos(angle)
    sin = np.sin(angle)
    x_forward = np.zeros((2 * KPAD, NG))
    x_forward[:HALF] = cos[:HALF]
    x_forward[KPAD : KPAD + HALF] = -sin[:HALF]
    x_inverse = x_forward.T
    z_forward = np.zeros((2 * LANES, 2 * LANES))
    z_inverse = np.zeros((2 * LANES, 2 * LANES))
    for table, sign in ((z_forward, 1.0), (z_inverse, -1.0)):
        table[:NG, :NG] = cos
        table[:NG, LANES : LANES + NG] = -sign * sin
        table[LANES : LANES + NG, :NG] = sign * sin
        table[LANES : LANES + NG, LANES : LANES + NG] = cos
    y_forward = np.block([[cos, sin], [-sin, cos]])
    y_inverse = np.block([[cos, -sin], [sin, cos]])
    symbol = 4.0 * np.sin(math.pi / NG * a) ** 2
    denominator = (
        screening + symbol[:HALF, None, None] + symbol[None, :, None] + symbol[None, None, :]
    )
    weight = np.where((a[:HALF] == 0) | (a[:HALF] == NG // 2), 1.0, 2.0) / float(NG**3)
    kernel = weight[:, None, None] / denominator
    kernel[0, 0, 0] = 0.0
    padded = np.zeros((KPAD, NG, LANES))
    padded[:HALF, :, :NG] = kernel
    padded = padded.reshape(PAIRS, 2, NG, LANES).transpose(0, 2, 1, 3)
    padded = padded.reshape(PAIRS, NG, 2 * LANES)
    narrow = [
        jnp.asarray(t.astype(np.float32)).astype(jnp.bfloat16)
        for t in (x_forward, x_inverse, z_forward, z_inverse, y_forward, y_inverse)
    ]
    return (*narrow, jnp.asarray(padded.astype(np.float32)))


def dot(a, b):
    return jnp.dot(a, b, preferred_element_type=jnp.float32)


def forward_x(grid, part_re, part_im, xf):
    table = xf[...]

    @pl.loop(0, NG // (2 * GROUP_Y))
    def _(step):
        for inner in range(GROUP_Y):
            y = (step * GROUP_Y + inner) * 2
            plane = jnp.concatenate(
                [grid[pl.ds(y + i, NG, stride=NG), :] for i in range(2)], axis=1
            ).astype(jnp.bfloat16)
            out = dot(table, plane)
            for i in range(2):
                lanes = slice(i * LANES, (i + 1) * LANES)
                part_re[pl.ds(y + i, KPAD, stride=NG), :] = out[:KPAD, lanes]
                part_im[pl.ds(y + i, KPAD, stride=NG), :] = out[KPAD:, lanes]


def restack(block):
    top, low = block[:NG], block[NG:]
    return jnp.concatenate(
        [
            jnp.concatenate([top[:, :LANES], low[:, :LANES]], axis=1),
            jnp.concatenate([top[:, LANES:], low[:, LANES:]], axis=1),
        ],
        axis=0,
    ).astype(jnp.bfloat16)


def middle(part_re, part_im, zf, zi, yf, yi, kern):
    @pl.loop(0, PAIRS // GROUP_K)
    def _(step):
        pairs = [step * GROUP_K + inner for inner in range(GROUP_K)]
        span = GROUP_K * 2 * NG
        rows = pl.ds(pl.multiple_of(step * span, 16), span)
        work = jnp.concatenate([part_re[rows, :], part_im[rows, :]], axis=1).astype(jnp.bfloat16)
        work = dot(work, zf[...])
        work = [restack(work[g * 2 * NG : (g + 1) * 2 * NG]) for g in range(GROUP_K)]
        third = []
        for w, p in zip(work, pairs):
            t = dot(yf[...], w)
            scale = kern[p]
            third.append(
                jnp.concatenate([t[:NG] * scale, t[NG:] * scale], axis=0).astype(jnp.bfloat16)
            )
        work = [restack(dot(yi[...], t)) for t in third]
        out = dot(jnp.concatenate(work, axis=0), zi[...])
        part_re[rows, :] = out[:, :LANES]
        part_im[rows, :] = out[:, LANES:]


def inverse_x(grid, part_re, part_im, xi):
    table = xi[...]

    @pl.loop(0, NG // (2 * GROUP_Y))
    def _(step):
        for inner in range(GROUP_Y):
            y = (step * GROUP_Y + inner) * 2
            plane = jnp.concatenate(
                [
                    jnp.concatenate(
                        [
                            part_re[pl.ds(y + i, KPAD, stride=NG), :],
                            part_im[pl.ds(y + i, KPAD, stride=NG), :],
                        ],
                        axis=0,
                    )
                    for i in range(2)
                ],
                axis=1,
            ).astype(jnp.bfloat16)
            out = dot(table, plane)
            for i in range(2):
                grid[pl.ds(y + i, NG, stride=NG), :] = out[:, i * LANES : (i + 1) * LANES]


def widen(flat, wide, rows_per_half):
    lane = lax.broadcasted_iota(jnp.int32, (GROUPS, LANES), 1)

    @pl.loop(0, 2)
    def _(half):
        source = half * rows_per_half
        target = half * (NG * NG // 2)
        for r in range(PER_ROWS):
            first, offset = divmod(r * NG, LANES)
            value = flat[pl.ds(source + first, GROUPS, stride=PER_FLAT), :]
            if offset + NG > LANES:
                after = flat[pl.ds(source + first + 1, GROUPS, stride=PER_FLAT), :]
                value = jnp.where(lane >= offset, value, after)
            if offset:
                value = pltpu.roll(value, LANES - offset, 1)
            wide[pl.ds(target + r, GROUPS, stride=PER_ROWS), :] = value


def narrow(wide, flat):
    lane = lax.broadcasted_iota(jnp.int32, (GROUPS, LANES), 1)

    @pl.loop(0, 2)
    def _(half):
        source = half * (NG * NG // 2)
        target = half * (GROUPS * PER_FLAT)
        for s in range(PER_FLAT):
            first, offset = divmod(s * LANES, NG)
            value = None
            start = -offset
            row = first
            while start < LANES:
                piece = wide[pl.ds(source + row, GROUPS, stride=PER_ROWS), :]
                if start % LANES:
                    piece = pltpu.roll(piece, start % LANES, 1)
                value = piece if value is None else jnp.where(lane >= start, piece, value)
                start += NG
                row += 1
            flat[pl.ds(target + s, GROUPS, stride=PER_FLAT), :] = value


def unpack(packed, flat):
    halves, pieces, rows, _ = packed.shape

    @pl.loop(0, halves)
    def _(half):
        @pl.loop(0, pieces)
        def _(piece):
            start = pl.multiple_of((half * pieces + piece) * rows, 16)
            flat[pl.ds(start, rows), :] = packed[half, piece].astype(jnp.float32)


def planes(work):
    @pl.loop(0, NG)
    def _(x):
        work(pl.ds(pl.multiple_of(x * NG, 8), NG))


def transform(grid, part_re, part_im, tables, fetch):
    xf, xi, zf, zi, yf, yi, kern = tables
    forward_x(grid, part_re, part_im, xf)
    if fetch is not None:
        fetch.wait()
    middle(part_re, part_im, zf, zi, yf, yi, kern)
    inverse_x(grid, part_re, part_im, xi)


def self_kernel(packed, *refs):
    tables, refs = refs[:7], refs[7:]
    term, own, flat, value, grid, part_re, part_im, kern, kern_sem = refs
    fetch = pltpu.make_async_copy(tables[6], kern, kern_sem)
    fetch.start()
    tables = (*tables[:6], kern)
    unpack(packed, flat)
    widen(flat, value, packed.shape[1] * packed.shape[2])

    @planes
    def _(rows):
        u = value[rows, :]
        own[rows, :] = u.astype(jnp.bfloat16)
        grid[rows, :] = u * u

    transform(grid, part_re, part_im, tables, fetch)

    @planes
    def _(rows):
        term[rows, :] = grid[rows, :] * value[rows, :]


def pair_kernel(bond_keep, own, so_far, lower, upper, *refs):
    tables, refs = refs[:7], refs[7:]
    out, flat, value, grid, part_re, part_im, kern, kern_sem, total = refs
    fetch = pltpu.make_async_copy(tables[6], kern, kern_sem)
    fetch.start()
    tables = (*tables[:6], kern)
    position = lax.axis_index("band") * lax.axis_size("grid") + lax.axis_index("grid")
    orbits = bond_keep.shape[0]
    for which, packed in enumerate((lower, upper)):
        unpack(packed, flat)
        widen(flat, value, packed.shape[1] * packed.shape[2])

        @planes
        def _(rows):
            grid[rows, :] = own[rows, :].astype(jnp.float32) * value[rows, :]

        transform(grid, part_re, part_im, tables, fetch if which == 0 else None)
        keep = bond_keep[lax.rem(position + which, orbits), 0].astype(jnp.float32)
        before = so_far if which == 0 else total

        @planes
        def _(rows):
            total[rows, :] = before[rows, :] + grid[rows, :] * keep * value[rows, :]

    narrow(total, flat)
    half_rows = out.shape[1]
    for half in range(2):
        out[half] = flat[half * half_rows : (half + 1) * half_rows, :].astype(jnp.bfloat16)


def exchange_scratch(flat_rows):
    return [
        pltpu.VMEM((flat_rows, LANES), jnp.float32),
        pltpu.VMEM((NG * NG, LANES), jnp.float32),
        pltpu.VMEM((NG * NG, LANES), jnp.float32),
        pltpu.VMEM((KPAD * NG, LANES), jnp.float32),
        pltpu.VMEM((KPAD * NG, LANES), jnp.float32),
        pltpu.VMEM((PAIRS, NG, 2 * LANES), jnp.float32),
        pltpu.SemaphoreType.DMA,
    ]


def in_vmem(count):
    return [pl.BlockSpec(memory_space=pltpu.VMEM)] * count


def cost(count):
    return pl.CostEstimate(
        flops=count * 2_000_000_000, bytes_accessed=8_000_000, transcendentals=0
    )


PARAMS = pltpu.CompilerParams(vmem_limit_bytes=48 * 2**20)


def self_term(packed, tables):
    flat_rows = packed.size // LANES
    return pl.pallas_call(
        self_kernel,
        out_shape=(
            jax.ShapeDtypeStruct((NG * NG, LANES), jnp.float32),
            jax.ShapeDtypeStruct((NG * NG, LANES), jnp.bfloat16),
        ),
        in_specs=in_vmem(len(tables)) + [pl.BlockSpec(memory_space=pl.ANY)],
        out_specs=tuple(in_vmem(2)),
        scratch_shapes=exchange_scratch(flat_rows),
        compiler_params=PARAMS,
        cost_estimate=cost(1),
        name="self_term",
    )(packed, *tables)


def pair_terms(bond_keep, own, so_far, lower, upper, tables):
    flat_rows = lower.size // LANES
    return pl.pallas_call(
        pair_kernel,
        out_shape=jax.ShapeDtypeStruct((2, GROUPS * PER_FLAT, LANES), jnp.bfloat16),
        in_specs=[pl.BlockSpec(memory_space=pltpu.SMEM)]
        + in_vmem(3 + len(tables))
        + [pl.BlockSpec(memory_space=pl.ANY)],
        out_specs=pl.BlockSpec(memory_space=pltpu.VMEM),
        scratch_shapes=exchange_scratch(flat_rows)
        + [pltpu.VMEM((NG * NG, LANES), jnp.float32)],
        compiler_params=PARAMS,
        cost_estimate=cost(2),
        name="pair_terms",
    )(bond_keep, own, so_far, lower, upper, *tables)


def localize_kernel(
    bands, cores, chunks, orb, mix, loc, recv, mixed, landed, whole, blended, sems, out_sems
):
    mol = lax.axis_index("mol")
    band = lax.axis_index("band")
    core = lax.axis_index("grid")
    me = band * cores + core
    devices = bands * cores
    held = orb.shape[0]
    orbits = held * bands
    rows = orb.shape[2] // chunks
    mesh_id = pl.DeviceIdType.MESH

    barrier = pltpu.get_barrier_semaphore()

    @pl.loop(1, devices)
    def _(k):
        peer = lax.rem(me + k, devices)
        pl.semaphore_signal(
            barrier,
            inc=1,
            device_id=(mol, peer // cores, lax.rem(peer, cores)),
            device_id_type=mesh_id,
        )

    pl.semaphore_wait(barrier, devices - 1)

    def first(q, k, sender):
        span = pl.ds(q * rows, rows)
        peer = lax.rem(band + k, bands)
        return pltpu.make_async_remote_copy(
            src_ref=orb.at[:, peer, span],
            dst_ref=recv.at[q, sender],
            send_sem=sems.at[0, q, peer],
            recv_sem=sems.at[1, q, sender],
            device_id=(mol, peer, core),
            device_id_type=mesh_id,
        )

    def second(q, k, sender):
        peer = lax.rem(me + k, devices)
        sender_band, sender_core = sender // cores, lax.rem(sender, cores)
        return pltpu.make_async_remote_copy(
            src_ref=mixed.at[q, peer],
            dst_ref=landed.at[sender_core, sender_band, pl.ds(q * rows, rows)],
            send_sem=out_sems.at[0, q, peer],
            recv_sem=out_sems.at[1, q, sender],
            device_id=(mol, peer // cores, lax.rem(peer, cores)),
            device_id_type=mesh_id,
        )

    for q in range(chunks):

        @pl.loop(1, bands)
        def _(k):
            first(q, k, band).start()

    for q in range(chunks):
        for h in range(held):
            start = pl.multiple_of((band * held + h) * rows, 16)
            whole[pl.ds(start, rows), :] = orb[h, band, pl.ds(q * rows, rows), :].astype(
                jnp.float32
            )

        @pl.loop(1, bands)
        def _(k):
            sender = lax.rem(band + k, bands)
            first(q, k, sender).wait_recv()
            for h in range(held):
                start = pl.multiple_of((sender * held + h) * rows, 16)
                whole[pl.ds(start, rows), :] = recv[q, sender, h].astype(jnp.float32)

        table = mix[...]

        @pl.loop(0, rows // 8)
        def _(step):
            for inner in range(4):
                r = step * 8 + inner * 2
                block = jnp.concatenate(
                    [whole[pl.ds(r + i, orbits, stride=rows), :] for i in range(2)], axis=1
                ).astype(jnp.bfloat16)
                out = dot(table, block)
                for i in range(2):
                    blended[pl.ds(r + i, orbits, stride=rows), :] = out[
                        :, i * LANES : (i + 1) * LANES
                    ]

        @pl.loop(0, orbits)
        def _(i):
            start = pl.multiple_of(i * rows, 16)
            mixed[q, i] = blended[pl.ds(start, rows), :].astype(jnp.bfloat16)

        @pl.loop(1, devices)
        def _(k):
            second(q, k, me).start()

        landed[core, band, pl.ds(q * rows, rows)] = mixed[q, me]

    for q in range(chunks):

        @pl.loop(1, devices)
        def _(k):
            second(q, k, lax.rem(me + k, devices)).wait_recv()

    loc[...] = landed[...]
    for q in range(chunks):

        @pl.loop(1, bands)
        def _(k):
            first(q, k, band).wait_send()

        @pl.loop(1, devices)
        def _(k):
            second(q, k, me).wait_send()


def localize(orb, mix, cores):
    held, bands, rows, _ = orb.shape
    orbits = held * bands
    chunks = 3 if rows % 48 == 0 else 1
    part = rows // chunks
    return pl.pallas_call(
        functools.partial(localize_kernel, bands, cores, chunks),
        out_shape=jax.ShapeDtypeStruct((cores, bands, rows, LANES), jnp.bfloat16),
        in_specs=in_vmem(2),
        out_specs=pl.BlockSpec(memory_space=pltpu.VMEM),
        scratch_shapes=[
            pltpu.VMEM((chunks, bands, held, part, LANES), jnp.bfloat16),
            pltpu.VMEM((chunks, orbits, part, LANES), jnp.bfloat16),
            pltpu.VMEM((cores, bands, rows, LANES), jnp.bfloat16),
            pltpu.VMEM((orbits * part, LANES), jnp.float32),
            pltpu.VMEM((orbits * part, LANES), jnp.float32),
            pltpu.SemaphoreType.DMA((2, chunks, bands)),
            pltpu.SemaphoreType.DMA((2, chunks, bands * cores)),
        ],
        compiler_params=pltpu.CompilerParams(
            collective_id=0, has_side_effects=True, vmem_limit_bytes=32 * 2**20
        ),
        name="localize",
    )(orb, mix)


def mixing_matrix(group_order, localizer):
    groups, width, _ = localizer.shape
    orbits = group_order.shape[0]
    pick = (group_order[:, None] == jnp.arange(orbits, dtype=jnp.int32)[None, :]).astype(
        jnp.bfloat16
    )
    pick = pick.reshape(groups, width, orbits)
    half = jnp.einsum("gab,gbj->gaj", localizer, pick, preferred_element_type=jnp.float32)
    return jnp.einsum(
        "gai,gaj->ij", pick, half.astype(jnp.bfloat16), preferred_element_type=jnp.float32
    ).astype(jnp.bfloat16)


def body(orbitals, group_order, localizer, bond_keep):
    bands = lax.axis_size("band")
    cores = lax.axis_size("grid")
    held, span = orbitals.shape
    flat_rows = span // LANES
    rows = -(-flat_rows // (bands * 16)) * 16
    orb = orbitals.reshape(held, flat_rows, LANES)
    orb = jnp.pad(orb, ((0, 0), (0, rows * bands - flat_rows), (0, 0)))
    orb = orb.reshape(held, bands, rows, LANES)
    packed = localize(orb, mixing_matrix(group_order, localizer), cores)
    tables = build_tables()
    lower = from_behind(packed, ("band", "grid"), 1)
    upper = from_behind(packed, ("band", "grid"), -1)
    so_far, own = self_term(packed, tables)
    localized = packed.reshape(cores, bands * rows, LANES)[:, :flat_rows].reshape(1, -1)
    total = pair_terms(bond_keep, own, so_far, lower, upper, tables)
    return (localized, total.reshape(1, -1))


def solution(mesh):
    in_specs = (P(("mol", "band"), "grid"), P("mol"), P("mol", None, None), P("mol", None))
    out_specs = (P(("mol", "band", "grid"), None), P(("mol", "band", "grid"), None))
    return jax.shard_map(body, mesh=mesh, in_specs=in_specs, out_specs=out_specs, check_vma=False)
```

```python
import functools
import math

import jax
import jax.numpy as jnp
import numpy as np
from jax import lax
from jax.experimental import pallas as pl
from jax.experimental.pallas import tpu as pltpu
from jax.sharding import PartitionSpec as P

NG = 72
LANES = 128
HALF = NG // 2 + 1
KPAD = 40
PAIRS = KPAD // 2
GROUP_K = 5
GROUP_Y = 6
PER_FLAT = 9
PER_ROWS = 16
GROUPS = NG**3 // (2 * PER_FLAT * LANES)

screening = 0.0625


def build_tables():
    a = np.arange(NG)
    angle = 2.0 * math.pi / NG * ((a[:, None] * a[None, :]) % NG)
    cos = np.cos(angle)
    sin = np.sin(angle)
    x_forward = np.zeros((2 * KPAD, NG))
    x_forward[:HALF] = cos[:HALF]
    x_forward[KPAD : KPAD + HALF] = -sin[:HALF]
    x_inverse = x_forward.T
    z_forward = np.zeros((2 * LANES, 2 * LANES))
    z_inverse = np.zeros((2 * LANES, 2 * LANES))
    for table, sign in ((z_forward, 1.0), (z_inverse, -1.0)):
        table[:NG, :NG] = cos
        table[:NG, LANES : LANES + NG] = -sign * sin
        table[LANES : LANES + NG, :NG] = sign * sin
        table[LANES : LANES + NG, LANES : LANES + NG] = cos
    y_forward = np.block([[cos, sin], [-sin, cos]])
    y_inverse = np.block([[cos, -sin], [sin, cos]])
    symbol = 4.0 * np.sin(math.pi / NG * a) ** 2
    denominator = (
        screening + symbol[:HALF, None, None] + symbol[None, :, None] + symbol[None, None, :]
    )
    weight = np.where((a[:HALF] == 0) | (a[:HALF] == NG // 2), 1.0, 2.0) / float(NG**3)
    kernel = weight[:, None, None] / denominator
    kernel[0, 0, 0] = 0.0
    padded = np.zeros((KPAD, NG, LANES))
    padded[:HALF, :, :NG] = kernel
    padded = padded.reshape(PAIRS, 2, NG, LANES).transpose(0, 2, 1, 3)
    padded = padded.reshape(PAIRS, NG, 2 * LANES)
    narrow = [
        jnp.asarray(t.astype(np.float32)).astype(jnp.bfloat16)
        for t in (x_forward, x_inverse, z_forward, z_inverse, y_forward, y_inverse)
    ]
    return (*narrow, jnp.asarray(padded.astype(np.float32)))


def dot(a, b):
    return jnp.dot(a, b, preferred_element_type=jnp.float32)


def forward_x(left, right, part_re, part_im, xf):
    table = xf[...]

    @pl.loop(0, NG // (2 * GROUP_Y))
    def _(step):
        for inner in range(GROUP_Y):
            y = (step * GROUP_Y + inner) * 2
            plane = jnp.concatenate(
                [
                    left[pl.ds(y + i, NG, stride=NG), :] * right[pl.ds(y + i, NG, stride=NG), :]
                    for i in range(2)
                ],
                axis=1,
            ).astype(jnp.bfloat16)
            out = dot(table, plane)
            for i in range(2):
                lanes = slice(i * LANES, (i + 1) * LANES)
                part_re[pl.ds(y + i, KPAD, stride=NG), :] = out[:KPAD, lanes]
                part_im[pl.ds(y + i, KPAD, stride=NG), :] = out[KPAD:, lanes]


def restack(block):
    top, low = block[:NG], block[NG:]
    return jnp.concatenate(
        [
            jnp.concatenate([top[:, :LANES], low[:, :LANES]], axis=1),
            jnp.concatenate([top[:, LANES:], low[:, LANES:]], axis=1),
        ],
        axis=0,
    ).astype(jnp.bfloat16)


def middle(part_re, part_im, zf, zi, yf, yi, kern):
    @pl.loop(0, PAIRS // GROUP_K)
    def _(step):
        pairs = [step * GROUP_K + inner for inner in range(GROUP_K)]
        span = GROUP_K * 2 * NG
        rows = pl.ds(pl.multiple_of(step * span, 16), span)
        work = jnp.concatenate([part_re[rows, :], part_im[rows, :]], axis=1).astype(jnp.bfloat16)
        work = dot(work, zf[...])
        work = [restack(work[g * 2 * NG : (g + 1) * 2 * NG]) for g in range(GROUP_K)]
        third = []
        for w, p in zip(work, pairs):
            t = dot(yf[...], w)
            scale = kern[p]
            third.append(
                jnp.concatenate([t[:NG] * scale, t[NG:] * scale], axis=0).astype(jnp.bfloat16)
            )
        work = [restack(dot(yi[...], t)) for t in third]
        out = dot(jnp.concatenate(work, axis=0), zi[...])
        part_re[rows, :] = out[:, :LANES]
        part_im[rows, :] = out[:, LANES:]


def inverse_x(total, value, keep, part_re, part_im, xi):
    table = xi[...]

    @pl.loop(0, NG // (2 * GROUP_Y))
    def _(step):
        for inner in range(GROUP_Y):
            y = (step * GROUP_Y + inner) * 2
            plane = jnp.concatenate(
                [
                    jnp.concatenate(
                        [
                            part_re[pl.ds(y + i, KPAD, stride=NG), :],
                            part_im[pl.ds(y + i, KPAD, stride=NG), :],
                        ],
                        axis=0,
                    )
                    for i in range(2)
                ],
                axis=1,
            ).astype(jnp.bfloat16)
            out = dot(table, plane)
            for i in range(2):
                rows = pl.ds(y + i, NG, stride=NG)
                term = out[:, i * LANES : (i + 1) * LANES] * value[rows, :]
                if keep is not None:
                    term = total[rows, :] + keep * term
                total[rows, :] = term


def widen(flat, wide, rows_per_half):
    lane = lax.broadcasted_iota(jnp.int32, (GROUPS, LANES), 1)

    @pl.loop(0, 2)
    def _(half):
        source = half * rows_per_half
        target = half * (NG * NG // 2)
        for r in range(PER_ROWS):
            first, offset = divmod(r * NG, LANES)
            value = flat[pl.ds(source + first, GROUPS, stride=PER_FLAT), :]
            if offset + NG > LANES:
                after = flat[pl.ds(source + first + 1, GROUPS, stride=PER_FLAT), :]
                value = jnp.where(lane >= offset, value, after)
            if offset:
                value = pltpu.roll(value, LANES - offset, 1)
            wide[pl.ds(target + r, GROUPS, stride=PER_ROWS), :] = value


def narrow(wide, flat):
    lane = lax.broadcasted_iota(jnp.int32, (GROUPS, LANES), 1)

    @pl.loop(0, 2)
    def _(half):
        source = half * (NG * NG // 2)
        target = half * (GROUPS * PER_FLAT)
        for s in range(PER_FLAT):
            first, offset = divmod(s * LANES, NG)
            value = None
            start = -offset
            row = first
            while start < LANES:
                piece = wide[pl.ds(source + row, GROUPS, stride=PER_ROWS), :]
                if start % LANES:
                    piece = pltpu.roll(piece, start % LANES, 1)
                value = piece if value is None else jnp.where(lane >= start, piece, value)
                start += NG
                row += 1
            flat[pl.ds(target + s, GROUPS, stride=PER_FLAT), :] = value


def unpack(packed, flat):
    halves, pieces, rows, _ = packed.shape

    @pl.loop(0, halves)
    def _(half):
        @pl.loop(0, pieces)
        def _(piece):
            start = pl.multiple_of((half * pieces + piece) * rows, 16)
            flat[pl.ds(start, rows), :] = packed[half, piece].astype(jnp.float32)


def in_vmem(count):
    return [pl.BlockSpec(memory_space=pltpu.VMEM)] * count


def exchange_kernel(bands, cores, chunks, bond_keep, orb, mix, *refs):
    (xf, xi, zf, zi, yf, yi, spectral), refs = refs[:7], refs[7:]
    loc, out, recv, mixed, landed, whole, blended, partners, refs = *refs[:8], refs[8:]
    flat, own, value, total, part_re, part_im, kern = refs[:7]
    sems, out_sems, partner_sems, kern_sem = refs[7:]
    fetch = pltpu.make_async_copy(spectral, kern, kern_sem)
    fetch.start()
    mol = lax.axis_index("mol")
    band = lax.axis_index("band")
    core = lax.axis_index("grid")
    me = band * cores + core
    devices = bands * cores
    held = orb.shape[0]
    orbits = held * bands
    rows = orb.shape[2] // chunks
    mesh_id = pl.DeviceIdType.MESH

    barrier = pltpu.get_barrier_semaphore()

    @pl.loop(1, devices)
    def _(k):
        peer = lax.rem(me + k, devices)
        pl.semaphore_signal(
            barrier,
            inc=1,
            device_id=(mol, peer // cores, lax.rem(peer, cores)),
            device_id_type=mesh_id,
        )

    pl.semaphore_wait(barrier, devices - 1)

    def first(q, k, sender):
        span = pl.ds(q * rows, rows)
        peer = lax.rem(band + k, bands)
        return pltpu.make_async_remote_copy(
            src_ref=orb.at[:, peer, span],
            dst_ref=recv.at[q, sender],
            send_sem=sems.at[0, q, peer],
            recv_sem=sems.at[1, q, sender],
            device_id=(mol, peer, core),
            device_id_type=mesh_id,
        )

    def second(q, k, sender):
        peer = lax.rem(me + k, devices)
        sender_band, sender_core = sender // cores, lax.rem(sender, cores)
        return pltpu.make_async_remote_copy(
            src_ref=mixed.at[q, peer],
            dst_ref=landed.at[sender_core, sender_band, pl.ds(q * rows, rows)],
            send_sem=out_sems.at[0, q, peer],
            recv_sem=out_sems.at[1, q, sender],
            device_id=(mol, peer // cores, lax.rem(peer, cores)),
            device_id_type=mesh_id,
        )

    for q in range(chunks):

        @pl.loop(1, bands)
        def _(k):
            first(q, k, band).start()

    for q in range(chunks):
        for h in range(held):
            start = pl.multiple_of((band * held + h) * rows, 16)
            whole[pl.ds(start, rows), :] = orb[h, band, pl.ds(q * rows, rows), :].astype(
                jnp.float32
            )

        @pl.loop(1, bands)
        def _(k):
            sender = lax.rem(band + k, bands)
            first(q, k, sender).wait_recv()
            for h in range(held):
                start = pl.multiple_of((sender * held + h) * rows, 16)
                whole[pl.ds(start, rows), :] = recv[q, sender, h].astype(jnp.float32)

        table = mix[...]

        @pl.loop(0, rows // 8)
        def _(step):
            for inner in range(4):
                r = step * 8 + inner * 2
                block = jnp.concatenate(
                    [whole[pl.ds(r + i, orbits, stride=rows), :] for i in range(2)], axis=1
                ).astype(jnp.bfloat16)
                out = dot(table, block)
                for i in range(2):
                    blended[pl.ds(r + i, orbits, stride=rows), :] = out[
                        :, i * LANES : (i + 1) * LANES
                    ]

        @pl.loop(0, orbits)
        def _(i):
            start = pl.multiple_of(i * rows, 16)
            mixed[q, i] = blended[pl.ds(start, rows), :].astype(jnp.bfloat16)

        @pl.loop(1, devices)
        def _(k):
            second(q, k, me).start()

        landed[core, band, pl.ds(q * rows, rows)] = mixed[q, me]

    for q in range(chunks):

        @pl.loop(1, devices)
        def _(k):
            second(q, k, lax.rem(me + k, devices)).wait_recv()

    def partner(which):
        peer = lax.rem(me + (1, devices - 1)[which], devices)
        return pltpu.make_async_remote_copy(
            src_ref=landed,
            dst_ref=partners.at[which],
            send_sem=partner_sems.at[0, which],
            recv_sem=partner_sems.at[1, which],
            device_id=(mol, peer // cores, lax.rem(peer, cores)),
            device_id_type=mesh_id,
        )

    for which in range(2):
        partner(which).start()

    def potential(other, keep):
        forward_x(own, other, part_re, part_im, xf)
        if keep is None:
            fetch.wait()
        middle(part_re, part_im, zf, zi, yf, yi, kern)
        inverse_x(total, other, keep, part_re, part_im, xi)

    half_rows = out.shape[1]
    padded_rows = bands * rows * chunks
    unpack(landed, flat)
    widen(flat, own, padded_rows)
    for half in range(2):
        kept = flat[half * padded_rows : half * padded_rows + half_rows, :]
        loc[half] = kept.astype(jnp.bfloat16)
    potential(own, None)

    for which in range(2):
        partner(which).wait_recv()
        unpack(partners.at[which], flat)
        widen(flat, value, padded_rows)
        keep = bond_keep[lax.rem(me + which, devices), 0].astype(jnp.float32)
        potential(value, keep)

    narrow(total, flat)
    for half in range(2):
        out[half] = flat[half * half_rows : (half + 1) * half_rows, :].astype(jnp.bfloat16)

    for which in range(2):
        partner(which).wait_send()
    for q in range(chunks):

        @pl.loop(1, bands)
        def _(k):
            first(q, k, band).wait_send()

        @pl.loop(1, devices)
        def _(k):
            second(q, k, me).wait_send()


def exchange(bond_keep, orb, mix, tables, cores):
    held, bands, rows, _ = orb.shape
    orbits = held * bands
    chunks = 3 if rows % 48 == 0 else 1
    part = rows // chunks
    half = jax.ShapeDtypeStruct((2, GROUPS * PER_FLAT, LANES), jnp.bfloat16)
    grid = pltpu.VMEM((NG * NG, LANES), jnp.float32)
    spectrum = pltpu.VMEM((KPAD * NG, LANES), jnp.float32)
    return pl.pallas_call(
        functools.partial(exchange_kernel, bands, cores, chunks),
        out_shape=(half, half),
        in_specs=[pl.BlockSpec(memory_space=pltpu.SMEM)]
        + in_vmem(1 + len(tables))
        + [pl.BlockSpec(memory_space=pl.ANY)],
        out_specs=tuple(in_vmem(2)),
        scratch_shapes=[
            pltpu.VMEM((chunks, bands, held, part, LANES), jnp.bfloat16),
            pltpu.VMEM((chunks, orbits, part, LANES), jnp.bfloat16),
            pltpu.VMEM((cores, bands, rows, LANES), jnp.bfloat16),
            pltpu.VMEM((orbits * part, LANES), jnp.float32),
            pltpu.VMEM((orbits * part, LANES), jnp.float32),
            pltpu.VMEM((2, cores, bands, rows, LANES), jnp.bfloat16),
            pltpu.VMEM((cores * bands * rows, LANES), jnp.float32),
            grid,
            grid,
            grid,
            spectrum,
            spectrum,
            pltpu.VMEM((PAIRS, NG, 2 * LANES), jnp.float32),
            pltpu.SemaphoreType.DMA((2, chunks, bands)),
            pltpu.SemaphoreType.DMA((2, chunks, bands * cores)),
            pltpu.SemaphoreType.DMA((2, 2)),
            pltpu.SemaphoreType.DMA,
        ],
        compiler_params=pltpu.CompilerParams(
            collective_id=0, has_side_effects=True, vmem_limit_bytes=48 * 2**20
        ),
        name="exchange",
    )(bond_keep, orb, mix, *tables)


def mixing_matrix(group_order, localizer):
    groups, width, _ = localizer.shape
    orbits = group_order.shape[0]
    pick = (group_order[:, None] == jnp.arange(orbits, dtype=jnp.int32)[None, :]).astype(
        jnp.bfloat16
    )
    pick = pick.reshape(groups, width, orbits)
    half = jnp.einsum("gab,gbj->gaj", localizer, pick, preferred_element_type=jnp.float32)
    return jnp.einsum(
        "gai,gaj->ij", pick, half.astype(jnp.bfloat16), preferred_element_type=jnp.float32
    ).astype(jnp.bfloat16)


def body(orbitals, group_order, localizer, bond_keep):
    bands = lax.axis_size("band")
    cores = lax.axis_size("grid")
    held, span = orbitals.shape
    flat_rows = span // LANES
    rows = -(-flat_rows // (bands * 16)) * 16
    orb = orbitals.reshape(held, flat_rows, LANES)
    orb = jnp.pad(orb, ((0, 0), (0, rows * bands - flat_rows), (0, 0)))
    orb = orb.reshape(held, bands, rows, LANES)
    mix = mixing_matrix(group_order, localizer)
    localized, total = exchange(bond_keep, orb, mix, build_tables(), cores)
    return (localized.reshape(1, -1), total.reshape(1, -1))


def solution(mesh):
    in_specs = (P(("mol", "band"), "grid"), P("mol"), P("mol", None, None), P("mol", None))
    out_specs = (P(("mol", "band", "grid"), None), P(("mol", "band", "grid"), None))
    return jax.shard_map(body, mesh=mesh, in_specs=in_specs, out_specs=out_specs, check_vma=False)
```

```python
import functools
import math

import jax
import jax.numpy as jnp
import numpy as np
from jax import lax
from jax.experimental import pallas as pl
from jax.experimental.pallas import tpu as pltpu
from jax.sharding import PartitionSpec as P

NG = 72
LANES = 128
HALF = NG // 2 + 1
KPAD = 40
PAIRS = KPAD // 2
GROUP_K = 10
GROUP_Y = 9
PER_FLAT = 9
PER_ROWS = 16
GROUPS = NG**3 // (2 * PER_FLAT * LANES)

screening = 0.0625


def build_tables():
    a = np.arange(NG)
    angle = 2.0 * math.pi / NG * ((a[:, None] * a[None, :]) % NG)
    cos = np.cos(angle)
    sin = np.sin(angle)
    x_forward = np.zeros((2 * KPAD, NG))
    x_forward[:HALF] = cos[:HALF]
    x_forward[KPAD : KPAD + HALF] = -sin[:HALF]
    x_inverse = x_forward.T
    z_forward = np.zeros((2 * LANES, 2 * LANES))
    z_inverse = np.zeros((2 * LANES, 2 * LANES))
    for table, sign in ((z_forward, 1.0), (z_inverse, -1.0)):
        table[:NG, :NG] = cos
        table[:NG, LANES : LANES + NG] = -sign * sin
        table[LANES : LANES + NG, :NG] = sign * sin
        table[LANES : LANES + NG, LANES : LANES + NG] = cos
    y_forward = np.block([[cos, sin], [-sin, cos]])
    y_inverse = np.block([[cos, -sin], [sin, cos]])
    symbol = 4.0 * np.sin(math.pi / NG * a) ** 2
    denominator = (
        screening + symbol[:HALF, None, None] + symbol[None, :, None] + symbol[None, None, :]
    )
    weight = np.where((a[:HALF] == 0) | (a[:HALF] == NG // 2), 1.0, 2.0) / float(NG**3)
    kernel = weight[:, None, None] / denominator
    kernel[0, 0, 0] = 0.0
    padded = np.zeros((KPAD, NG, LANES))
    padded[:HALF, :, :NG] = kernel
    padded = padded.reshape(PAIRS, 2, NG, LANES).transpose(0, 2, 1, 3)
    padded = padded.reshape(PAIRS, NG, 2 * LANES)
    narrow = [
        jnp.asarray(t.astype(np.float32)).astype(jnp.bfloat16)
        for t in (x_forward, x_inverse, z_forward, z_inverse, y_forward, y_inverse)
    ]
    return (*narrow, jnp.asarray(padded.astype(np.float32)))


def dot(a, b):
    return jnp.dot(a, b, preferred_element_type=jnp.float32)


def forward_x(left, right, part_re, part_im, xf):
    table = xf[...]

    @pl.loop(0, NG // (2 * GROUP_Y))
    def _(step):
        for inner in range(GROUP_Y):
            y = (step * GROUP_Y + inner) * 2
            plane = jnp.concatenate(
                [
                    left[pl.ds(y + i, NG, stride=NG), :] * right[pl.ds(y + i, NG, stride=NG), :]
                    for i in range(2)
                ],
                axis=1,
            ).astype(jnp.bfloat16)
            out = dot(table, plane)
            for i in range(2):
                lanes = slice(i * LANES, (i + 1) * LANES)
                part_re[pl.ds(y + i, KPAD, stride=NG), :] = out[:KPAD, lanes]
                part_im[pl.ds(y + i, KPAD, stride=NG), :] = out[KPAD:, lanes]


def restack(block):
    top, low = block[:NG], block[NG:]
    return jnp.concatenate(
        [
            jnp.concatenate([top[:, :LANES], low[:, :LANES]], axis=1),
            jnp.concatenate([top[:, LANES:], low[:, LANES:]], axis=1),
        ],
        axis=0,
    ).astype(jnp.bfloat16)


def middle(part_re, part_im, zf, zi, yf, yi, kern):
    @pl.loop(0, PAIRS // GROUP_K)
    def _(step):
        pairs = [step * GROUP_K + inner for inner in range(GROUP_K)]
        span = GROUP_K * 2 * NG
        rows = pl.ds(pl.multiple_of(step * span, 16), span)
        work = jnp.concatenate([part_re[rows, :], part_im[rows, :]], axis=1).astype(jnp.bfloat16)
        work = dot(work, zf[...])
        work = [restack(work[g * 2 * NG : (g + 1) * 2 * NG]) for g in range(GROUP_K)]
        third = []
        for w, p in zip(work, pairs):
            t = dot(yf[...], w)
            scale = kern[p]
            third.append(
                jnp.concatenate([t[:NG] * scale, t[NG:] * scale], axis=0).astype(jnp.bfloat16)
            )
        work = [restack(dot(yi[...], t)) for t in third]
        out = dot(jnp.concatenate(work, axis=0), zi[...])
        part_re[rows, :] = out[:, :LANES]
        part_im[rows, :] = out[:, LANES:]


def inverse_x(total, value, keep, part_re, part_im, xi):
    table = xi[...]

    @pl.loop(0, NG // (2 * GROUP_Y))
    def _(step):
        for inner in range(GROUP_Y):
            y = (step * GROUP_Y + inner) * 2
            plane = jnp.concatenate(
                [
                    jnp.concatenate(
                        [
                            part_re[pl.ds(y + i, KPAD, stride=NG), :],
                            part_im[pl.ds(y + i, KPAD, stride=NG), :],
                        ],
                        axis=0,
                    )
                    for i in range(2)
                ],
                axis=1,
            ).astype(jnp.bfloat16)
            out = dot(table, plane)
            for i in range(2):
                rows = pl.ds(y + i, NG, stride=NG)
                term = out[:, i * LANES : (i + 1) * LANES] * value[rows, :]
                if keep is not None:
                    term = total[rows, :] + keep * term
                total[rows, :] = term


def widen(flat, wide, rows_per_half):
    lane = lax.broadcasted_iota(jnp.int32, (GROUPS, LANES), 1)

    @pl.loop(0, 2)
    def _(half):
        source = half * rows_per_half
        target = half * (NG * NG // 2)
        for r in range(PER_ROWS):
            first, offset = divmod(r * NG, LANES)
            value = flat[pl.ds(source + first, GROUPS, stride=PER_FLAT), :]
            if offset + NG > LANES:
                after = flat[pl.ds(source + first + 1, GROUPS, stride=PER_FLAT), :]
                value = jnp.where(lane >= offset, value, after)
            if offset:
                value = pltpu.roll(value, LANES - offset, 1)
            wide[pl.ds(target + r, GROUPS, stride=PER_ROWS), :] = value


def narrow(wide, flat):
    lane = lax.broadcasted_iota(jnp.int32, (GROUPS, LANES), 1)

    @pl.loop(0, 2)
    def _(half):
        source = half * (NG * NG // 2)
        target = half * (GROUPS * PER_FLAT)
        for s in range(PER_FLAT):
            first, offset = divmod(s * LANES, NG)
            value = None
            start = -offset
            row = first
            while start < LANES:
                piece = wide[pl.ds(source + row, GROUPS, stride=PER_ROWS), :]
                if start % LANES:
                    piece = pltpu.roll(piece, start % LANES, 1)
                value = piece if value is None else jnp.where(lane >= start, piece, value)
                start += NG
                row += 1
            flat[pl.ds(target + s, GROUPS, stride=PER_FLAT), :] = value


def unpack(packed, flat):
    halves, pieces, rows, _ = packed.shape

    @pl.loop(0, halves)
    def _(half):
        @pl.loop(0, pieces)
        def _(piece):
            start = pl.multiple_of((half * pieces + piece) * rows, 16)
            flat[pl.ds(start, rows), :] = packed[half, piece].astype(jnp.float32)


def in_vmem(count):
    return [pl.BlockSpec(memory_space=pltpu.VMEM)] * count


def exchange_kernel(bands, cores, chunks, bond_keep, orb, mix, *refs):
    (xf, xi, zf, zi, yf, yi, spectral), refs = refs[:7], refs[7:]
    loc, out, recv, mixed, landed, whole, blended, partners, refs = *refs[:8], refs[8:]
    flat, own, value, total, part_re, part_im, kern = refs[:7]
    sems, out_sems, partner_sems, kern_sem = refs[7:]
    fetch = pltpu.make_async_copy(spectral, kern, kern_sem)
    fetch.start()
    mol = lax.axis_index("mol")
    band = lax.axis_index("band")
    core = lax.axis_index("grid")
    me = band * cores + core
    devices = bands * cores
    held = orb.shape[0]
    orbits = held * bands
    rows = orb.shape[2] // chunks
    mesh_id = pl.DeviceIdType.MESH

    barrier = pltpu.get_barrier_semaphore()

    @pl.loop(1, devices)
    def _(k):
        peer = lax.rem(me + k, devices)
        pl.semaphore_signal(
            barrier,
            inc=1,
            device_id=(mol, peer // cores, lax.rem(peer, cores)),
            device_id_type=mesh_id,
        )

    pl.semaphore_wait(barrier, devices - 1)

    def first(q, k, sender):
        span = pl.ds(q * rows, rows)
        peer = lax.rem(band + k, bands)
        return pltpu.make_async_remote_copy(
            src_ref=orb.at[:, peer, span],
            dst_ref=recv.at[q, sender],
            send_sem=sems.at[0, q, peer],
            recv_sem=sems.at[1, q, sender],
            device_id=(mol, peer, core),
            device_id_type=mesh_id,
        )

    def second(q, k, sender):
        peer = lax.rem(me + k, devices)
        sender_band, sender_core = sender // cores, lax.rem(sender, cores)
        return pltpu.make_async_remote_copy(
            src_ref=mixed.at[q, peer],
            dst_ref=landed.at[sender_core, sender_band, pl.ds(q * rows, rows)],
            send_sem=out_sems.at[0, q, peer],
            recv_sem=out_sems.at[1, q, sender],
            device_id=(mol, peer // cores, lax.rem(peer, cores)),
            device_id_type=mesh_id,
        )

    for q in range(chunks):

        @pl.loop(1, bands)
        def _(k):
            first(q, k, band).start()

    for q in range(chunks):
        for h in range(held):
            start = pl.multiple_of((band * held + h) * rows, 16)
            whole[pl.ds(start, rows), :] = orb[h, band, pl.ds(q * rows, rows), :].astype(
                jnp.float32
            )

        @pl.loop(1, bands)
        def _(k):
            sender = lax.rem(band + k, bands)
            first(q, k, sender).wait_recv()
            for h in range(held):
                start = pl.multiple_of((sender * held + h) * rows, 16)
                whole[pl.ds(start, rows), :] = recv[q, sender, h].astype(jnp.float32)

        table = mix[...]

        @pl.loop(0, rows // 8)
        def _(step):
            for inner in range(4):
                r = step * 8 + inner * 2
                block = jnp.concatenate(
                    [whole[pl.ds(r + i, orbits, stride=rows), :] for i in range(2)], axis=1
                ).astype(jnp.bfloat16)
                out = dot(table, block)
                for i in range(2):
                    blended[pl.ds(r + i, orbits, stride=rows), :] = out[
                        :, i * LANES : (i + 1) * LANES
                    ]

        @pl.loop(0, orbits)
        def _(i):
            start = pl.multiple_of(i * rows, 16)
            mixed[q, i] = blended[pl.ds(start, rows), :].astype(jnp.bfloat16)

        @pl.loop(1, devices)
        def _(k):
            second(q, k, me).start()

        landed[core, band, pl.ds(q * rows, rows)] = mixed[q, me]

    for q in range(chunks):

        @pl.loop(1, devices)
        def _(k):
            second(q, k, lax.rem(me + k, devices)).wait_recv()

    def partner(which):
        peer = lax.rem(me + (1, devices - 1)[which], devices)
        return pltpu.make_async_remote_copy(
            src_ref=landed,
            dst_ref=partners.at[which],
            send_sem=partner_sems.at[0, which],
            recv_sem=partner_sems.at[1, which],
            device_id=(mol, peer // cores, lax.rem(peer, cores)),
            device_id_type=mesh_id,
        )

    for which in range(2):
        partner(which).start()

    def potential(other, keep):
        forward_x(own, other, part_re, part_im, xf)
        if keep is None:
            fetch.wait()
        middle(part_re, part_im, zf, zi, yf, yi, kern)
        inverse_x(total, other, keep, part_re, part_im, xi)

    half_rows = out.shape[1]
    padded_rows = bands * rows * chunks
    unpack(landed, flat)
    widen(flat, own, padded_rows)
    for half in range(2):
        kept = flat[half * padded_rows : half * padded_rows + half_rows, :]
        loc[half] = kept.astype(jnp.bfloat16)
    potential(own, None)

    for which in range(2):
        partner(which).wait_recv()
        unpack(partners.at[which], flat)
        widen(flat, value, padded_rows)
        keep = bond_keep[lax.rem(me + which, devices), 0].astype(jnp.float32)
        potential(value, keep)

    narrow(total, flat)
    for half in range(2):
        out[half] = flat[half * half_rows : (half + 1) * half_rows, :].astype(jnp.bfloat16)

    for which in range(2):
        partner(which).wait_send()
    for q in range(chunks):

        @pl.loop(1, bands)
        def _(k):
            first(q, k, band).wait_send()

        @pl.loop(1, devices)
        def _(k):
            second(q, k, me).wait_send()


def exchange(bond_keep, orb, mix, tables, cores):
    held, bands, rows, _ = orb.shape
    orbits = held * bands
    chunks = 2 if rows % 32 == 0 else 1
    part = rows // chunks
    half = jax.ShapeDtypeStruct((2, GROUPS * PER_FLAT, LANES), jnp.bfloat16)
    grid = pltpu.VMEM((NG * NG, LANES), jnp.float32)
    spectrum = pltpu.VMEM((KPAD * NG, LANES), jnp.float32)
    return pl.pallas_call(
        functools.partial(exchange_kernel, bands, cores, chunks),
        out_shape=(half, half),
        in_specs=[pl.BlockSpec(memory_space=pltpu.SMEM)]
        + in_vmem(1 + len(tables))
        + [pl.BlockSpec(memory_space=pl.ANY)],
        out_specs=tuple(in_vmem(2)),
        scratch_shapes=[
            pltpu.VMEM((chunks, bands, held, part, LANES), jnp.bfloat16),
            pltpu.VMEM((chunks, orbits, part, LANES), jnp.bfloat16),
            pltpu.VMEM((cores, bands, rows, LANES), jnp.bfloat16),
            pltpu.VMEM((orbits * part, LANES), jnp.float32),
            pltpu.VMEM((orbits * part, LANES), jnp.float32),
            pltpu.VMEM((2, cores, bands, rows, LANES), jnp.bfloat16),
            pltpu.VMEM((cores * bands * rows, LANES), jnp.float32),
            grid,
            grid,
            grid,
            spectrum,
            spectrum,
            pltpu.VMEM((PAIRS, NG, 2 * LANES), jnp.float32),
            pltpu.SemaphoreType.DMA((2, chunks, bands)),
            pltpu.SemaphoreType.DMA((2, chunks, bands * cores)),
            pltpu.SemaphoreType.DMA((2, 2)),
            pltpu.SemaphoreType.DMA,
        ],
        compiler_params=pltpu.CompilerParams(
            collective_id=0, has_side_effects=True, vmem_limit_bytes=48 * 2**20
        ),
        name="exchange",
    )(bond_keep, orb, mix, *tables)


def mixing_matrix(group_order, localizer):
    groups, width, _ = localizer.shape
    orbits = group_order.shape[0]
    pick = (group_order[:, None] == jnp.arange(orbits, dtype=jnp.int32)[None, :]).astype(
        jnp.bfloat16
    )
    pick = pick.reshape(groups, width, orbits)
    half = jnp.einsum("gab,gbj->gaj", localizer, pick, preferred_element_type=jnp.float32)
    return jnp.einsum(
        "gai,gaj->ij", pick, half.astype(jnp.bfloat16), preferred_element_type=jnp.float32
    ).astype(jnp.bfloat16)


def body(orbitals, group_order, localizer, bond_keep):
    bands = lax.axis_size("band")
    cores = lax.axis_size("grid")
    held, span = orbitals.shape
    flat_rows = span // LANES
    rows = -(-flat_rows // (bands * 16)) * 16
    orb = orbitals.reshape(held, flat_rows, LANES)
    orb = jnp.pad(orb, ((0, 0), (0, rows * bands - flat_rows), (0, 0)))
    orb = orb.reshape(held, bands, rows, LANES)
    mix = mixing_matrix(group_order, localizer)
    localized, total = exchange(bond_keep, orb, mix, build_tables(), cores)
    return (localized.reshape(1, -1), total.reshape(1, -1))


def solution(mesh):
    in_specs = (P(("mol", "band"), "grid"), P("mol"), P("mol", None, None), P("mol", None))
    out_specs = (P(("mol", "band", "grid"), None), P(("mol", "band", "grid"), None))
    return jax.shard_map(body, mesh=mesh, in_specs=in_specs, out_specs=out_specs, check_vma=False)
```
